32 devices in a mesh: dp: 4 (over x, core), fsdp: 2 (over y), ctx: 4 (over z).
Axes of the slice: x: 2, y: 2, z: 4, core: 2. Of those that a mesh axis runs over, the one named last changes fastest.
Arguments:
- box_hidden_states: bfloat16 [8, 2048, 8192], P(('dp', 'fsdp'), 'ctx'), may hold values from -60 to 60
- box_token_positions: int32 [8, 2048], P(('dp', 'fsdp')), may hold values from 0 to 8191, as said below
- document_lengths: int32 [8, 3], P(('dp', 'fsdp')), may hold values from 512 to 7168, as said below
- successors: int32 [8, 2048], P(('dp', 'fsdp'), 'ctx'), may hold values from 0 to 2047, as said below
- fixed_key_matrix: bfloat16 [8192, 1024], P('fsdp'), may hold values from -0.0625 to 0.0625
- adapter_down: bfloat16 [8192, 16], replicated, may hold values from -0.0625 to 0.0625
- adapter_up: bfloat16 [16, 1024], replicated, may hold values from -1.5 to 1.5
- pointer_query_map: bfloat16 [1024, 64], replicated, may hold values from -0.1875 to 0.1875
- pointer_key_map: bfloat16 [1024, 64], replicated, may hold values from -0.1875 to 0.1875
Outputs:
- grad_down: float32 [8192, 16], P('fsdp')
- up_gradient: float32 [16, 1024], replicated
- grad_query: float32 [1024, 64], replicated
- grad_key: float32 [1024, 64], replicated
- mean_loss: float32 [], replicated
The draws below stay inside these ranges and needn't reach their ends.
Inputs may be any that keep to these rules, and one draw needn't show every extreme that they name: `box_token_positions`: each row is increasing; entries k * 512 to (k + 1) * 512 - 1 lie in positions k * 2048 to (k + 1) * 2048 - 1. `document_lengths`: each row holds multiples of 512 that sum to 8192. `successors`: the index of a box token of the same sequence and the same document as the query; the query itself only where it is the document's only box token or so drawn.
All inputs are finite; a program needn't handle non-finite values.
Results may differ from the reference program's by a relative error of at most 0.012.
The reference program's roundings to bfloat16 on the way count: a program that leaves them out, or rounds other values in their place, can miss the bound.
Values may be sent and summed in bfloat16 or wider, within the bound.
A program may use at most 128 MiB of HBM per device.

```python
import math
import jax
import jax.numpy as jnp
from jax import lax

MODEL_WIDTH = 8192
KEY_WIDTH = 1024
ADAPTER_RANK = 16
PD = 64
NDOC = 3
NBOX_DEV = 512
TOK_DEV = 2048
NBOX = 2048
SEQS = 8
N_CTX = 4


def box_layout(key):
    base = jax.random.fold_in(key, 11)
    key_pos, key_cut, key_pick = jax.random.split(base, 3)
    blocks = SEQS * N_CTX
    pos_keys = jax.random.split(key_pos, blocks)
    perms = jax.vmap(lambda k: jax.random.permutation(k, TOK_DEV - 2))(pos_keys)
    inner = perms[:, :NBOX_DEV - 2] + 1
    first = jnp.zeros((blocks, 1), jnp.int32)
    last = jnp.full((blocks, 1), TOK_DEV - 1, jnp.int32)
    chosen = jnp.sort(jnp.concatenate([first, inner.astype(jnp.int32), last], axis=1), axis=1)
    offsets = jnp.arange(blocks, dtype=jnp.int32) % N_CTX * TOK_DEV
    token_positions = (chosen + offsets[:, None]).reshape(SEQS, NBOX).astype(jnp.int32)
    units = 4 * N_CTX
    grain = TOK_DEV // 4
    cut_keys = jax.random.split(key_cut, SEQS)
    cuts = jax.vmap(lambda k: jax.random.permutation(k, units - 1))(cut_keys)[:, :NDOC - 1] + 1
    cuts = jnp.sort(cuts, axis=1).astype(jnp.int32)
    fixed = jnp.arange(1, NDOC, dtype=jnp.int32)[None, :]
    first_seq = (jnp.arange(SEQS, dtype=jnp.int32) == 0)[:, None]
    cuts = jnp.where(first_seq, fixed, cuts).astype(jnp.int32)
    bounds = jnp.concatenate([jnp.zeros((SEQS, 1), jnp.int32), cuts, jnp.full((SEQS, 1), units, jnp.int32)], axis=1)
    length_list = ((bounds[:, 1:] - bounds[:, :-1]) * grain).astype(jnp.int32)
    ends = jnp.cumsum(length_list, axis=1)
    segment = jnp.sum((token_positions[:, :, None] >= ends[:, None, :NDOC - 1]).astype(jnp.int32), axis=2)
    onehot = (segment[:, :, None] == jnp.arange(NDOC, dtype=jnp.int32)[None, None, :]).astype(jnp.int32)
    counts = jnp.sum(onehot, axis=1)
    starts = jnp.cumsum(counts, axis=1) - counts
    lower = jnp.sum(onehot * starts[:, None, :], axis=2)
    number = jnp.sum(onehot * counts[:, None, :], axis=2)
    raw = jax.random.randint(key_pick, (SEQS, NBOX), 0, 1 << 20, dtype=jnp.int32)
    offset = raw % number
    column = jnp.arange(NBOX, dtype=jnp.int32)[None, :]
    offset = jnp.where(column == 0, 0, offset)
    offset = jnp.where(column == NBOX - 1, number - 1, offset)
    target_boxes = (lower + offset).astype(jnp.int32)
    return (token_positions, length_list, target_boxes)


def draw_box_token_positions(key, part):
    return box_layout(key)[0]


def draw_document_lengths(key, part):
    return box_layout(key)[1]


def draw_successors(key, part):
    return box_layout(key)[2]


def draw_box_hidden_states(key, part):
    key_a, key_b = jax.random.split(jax.random.fold_in(key, 5), 2)
    base = jnp.clip(jax.random.normal(key_a, (SEQS, NBOX, MODEL_WIDTH), jnp.float32), -6.0, 6.0)
    rows = jnp.exp(jax.random.uniform(key_b, (SEQS, NBOX, 1), jnp.float32, math.log(0.5), math.log(2.0)))
    values = base * rows
    return jnp.clip(values, -60.0, 60.0).astype(jnp.bfloat16)


def block_scale(key, dims, cuts, smallest, high):
    loudness, own = 1.0, jax.random.fold_in(key, 6)
    for dim, shards_of in cuts:
        steps = jnp.exp(jax.random.uniform(jax.random.fold_in(own, dim), (shards_of,), jnp.float32, smallest / len(cuts), high / len(cuts)))
        loudness = loudness * jnp.repeat(steps, dims[dim] // shards_of).reshape([-1 if axis == dim else 1 for axis in range(len(dims))])
    return loudness


def noise(own_key, extent, deviation, limit, cuts=(), held_as=jnp.bfloat16):
    values = deviation * jax.random.normal(own_key, extent, jnp.float32)
    if cuts:
        values = values * block_scale(own_key, extent, cuts, -0.22, 0.18)
    return jnp.clip(values, -limit, limit).astype(held_as)


def setup_inputs(seed: int = 0) -> dict:
    seeds = jax.random.split(jax.random.key(seed), 10)
    box_hidden_states = draw_box_hidden_states(jax.random.fold_in(seeds[9], 71), 0)
    box_token_positions = draw_box_token_positions(jax.random.fold_in(seeds[9], 71), 0)
    document_lengths = draw_document_lengths(jax.random.fold_in(seeds[9], 71), 0)
    successors = draw_successors(jax.random.fold_in(seeds[9], 71), 0)
    fixed_key_matrix = noise(seeds[4], (MODEL_WIDTH, KEY_WIDTH), MODEL_WIDTH ** -0.5, 0.0625, ((0, 2),))
    adapter_down = noise(seeds[5], (MODEL_WIDTH, ADAPTER_RANK), MODEL_WIDTH ** -0.5, 0.0625)
    adapter_up = noise(seeds[6], (ADAPTER_RANK, KEY_WIDTH), ADAPTER_RANK ** -0.5, 1.5)
    pointer_query_map = noise(seeds[7], (KEY_WIDTH, PD), KEY_WIDTH ** -0.5, 0.1875)
    pointer_key_map = noise(seeds[8], (KEY_WIDTH, PD), KEY_WIDTH ** -0.5, 0.1875)
    return {"box_hidden_states": box_hidden_states, "box_token_positions": box_token_positions, "document_lengths": document_lengths, "successors": successors, "fixed_key_matrix": fixed_key_matrix, "adapter_down": adapter_down, "adapter_up": adapter_up, "pointer_query_map": pointer_query_map, "pointer_key_map": pointer_key_map}


ADAPTER_SCALE = 0.5

def precise_rows(left, right):
    return lax.dot_general(left.astype(jnp.float32), right.astype(jnp.float32), (((0,), (0,)), ((), ())), precision=lax.Precision.HIGHEST, preferred_element_type=jnp.float32)

def precise_columns(left, right):
    return lax.dot_general(left.astype(jnp.float32), right.astype(jnp.float32), (((1,), (1,)), ((), ())), precision=lax.Precision.HIGHEST, preferred_element_type=jnp.float32)

def single_sequence(hidden_states, token_positions, length_list, target_boxes, pointer_logits, adapter_pointer, adapter_down):
    scale = 1.0 / math.sqrt(PD)
    ends = jnp.cumsum(length_list)
    segment = lax.optimization_barrier(jnp.sum((token_positions[:, None] >= ends[None, :-1]).astype(jnp.int32), axis=1))
    narrow_rows = jnp.dot(hidden_states, adapter_down, preferred_element_type=jnp.float32).astype(jnp.bfloat16)
    blended_terms = (jnp.dot(hidden_states, pointer_logits, preferred_element_type=jnp.float32) + ADAPTER_SCALE * jnp.dot(narrow_rows, adapter_pointer, preferred_element_type=jnp.float32)).astype(jnp.bfloat16)
    queries = blended_terms[:, :PD]
    keys = blended_terms[:, PD:]
    scores = jnp.dot(queries, keys.T, preferred_element_type=jnp.float32) * scale
    same = segment[:, None] == segment[None, :]
    masked = jnp.where(same, scores, -jnp.inf)
    top = lax.optimization_barrier(jnp.max(masked, axis=1, keepdims=True))
    total = lax.optimization_barrier(jnp.sum(jnp.exp(masked - top), axis=1, keepdims=True))
    lse = top + jnp.log(total)
    column = jnp.arange(NBOX, dtype=jnp.int32)
    hit = column[None, :] == target_boxes[:, None]
    picked = lax.optimization_barrier(jnp.sum(jnp.where(hit, scores, 0.0), axis=1))
    loss = jnp.sum(lse[:, 0] - picked)
    prob = jnp.exp(masked - lse)
    weights = ((prob - hit.astype(jnp.float32)) * (scale * (1.0 / SEQS))).astype(jnp.bfloat16)
    grad_q = jnp.dot(weights, keys, preferred_element_type=jnp.float32).astype(jnp.bfloat16)
    grad_k = jnp.dot(weights.T, queries, preferred_element_type=jnp.float32).astype(jnp.bfloat16)
    paired_terms = jnp.concatenate([grad_q, grad_k], axis=1)
    narrow_gradient = (ADAPTER_SCALE * jnp.dot(paired_terms, adapter_pointer.T, preferred_element_type=jnp.float32)).astype(jnp.bfloat16)
    projection_gradient = jnp.dot(hidden_states.T, paired_terms, preferred_element_type=jnp.float32)
    narrow_rows_gradient = jnp.dot(narrow_rows.T, paired_terms, preferred_element_type=jnp.float32)
    grad_down = jnp.dot(hidden_states.T, narrow_gradient, preferred_element_type=jnp.float32)
    return (loss, grad_down, projection_gradient, narrow_rows_gradient)

def reference(box_hidden_states, box_token_positions, document_lengths, successors, fixed_key_matrix, adapter_down, adapter_up, pointer_query_map, pointer_key_map):
    pointer_heads = jnp.concatenate([pointer_query_map, pointer_key_map], axis=1)
    pointer_logits = jnp.dot(fixed_key_matrix, pointer_heads, preferred_element_type=jnp.float32).astype(jnp.bfloat16)
    adapter_pointer = jnp.dot(adapter_up, pointer_heads, preferred_element_type=jnp.float32).astype(jnp.bfloat16)

    def step(carry, index_value):
        final_result = single_sequence(box_hidden_states[index_value], box_token_positions[index_value], document_lengths[index_value], successors[index_value], pointer_logits, adapter_pointer, adapter_down)
        return (jax.tree.map(lambda a, b: a + b, carry, final_result), None)
    start = (jnp.zeros((), jnp.float32), jnp.zeros((MODEL_WIDTH, ADAPTER_RANK), jnp.float32), jnp.zeros((MODEL_WIDTH, 2 * PD), jnp.float32), jnp.zeros((ADAPTER_RANK, 2 * PD), jnp.float32))
    totals, _ = lax.scan(step, start, jnp.arange(SEQS, dtype=jnp.int32))
    loss, grad_down, projection_gradient, narrow_rows_gradient = totals
    head_gradients = precise_rows(fixed_key_matrix, projection_gradient) + ADAPTER_SCALE * precise_rows(adapter_up, narrow_rows_gradient)
    up_gradient = ADAPTER_SCALE * precise_columns(narrow_rows_gradient, pointer_heads)
    return (grad_down, up_gradient, head_gradients[:, :PD], head_gradients[:, PD:], loss / (SEQS * NBOX))
```

```python
import functools
import math

import jax
import jax.numpy as jnp
from jax import lax
from jax.experimental import pallas as pl
from jax.experimental.pallas import tpu as pltpu
from jax.sharding import PartitionSpec as P

ADAPTER_SCALE = 0.5
BF = jnp.bfloat16
F32 = jnp.float32


def mm(a, b):
    return lax.dot_general(a, b, (((1,), (0,)), ((), ())), preferred_element_type=F32)


def mm_t(a, b):
    return lax.dot_general(a, b, (((1,), (1,)), ((), ())), preferred_element_type=F32)


def at(start, size, unit):
    return pl.ds(pl.multiple_of(start, unit), size)


def kernel(
    D, F, C, seqs_all,
    h_hbm, k_hbm, down_t, up, heads, pos, lengths, succ,
    o_grad, o_up, o_down, o_loss,
    hbuf, kbuf, pbuf, acc, lowacc, bl, blt, keys_t, wts, seg_col, succ_col,
    gks, gkr, g_t, core_s, core_r, own, y_s, y_r, proj,
    pay, r1, p2, r2, p3, r3, fin, gd, gd_x, gd2, gd_r, gd_all,
    load_sem, send_sem, recv_sem,
):
    rows_all, rank = hbuf.shape[1], up.shape[0]
    count, width = hbuf.shape[0], bl.shape[1] // 2
    RF = rows_all // F
    PC = RF // 2
    SUB = PC // 2
    dp, f, ctx = lax.axis_index("dp"), lax.axis_index("fsdp"), lax.axis_index("ctx")
    par = lax.rem(dp, 2)
    mate = dp + 1 - 2 * par
    other = 1 - par

    loads = []

    def load(src, dst):
        cp = pltpu.make_async_copy(src, dst, load_sem.at[len(loads)])
        cp.start()
        loads.append(cp)
        return cp

    def krows(p, s):
        return at(p * PC + s * SUB, SUB, SUB)

    lk = [
        load(k_hbm.at[krows(p, s)], kbuf.at[krows(p, s)])
        for p in (par, other)
        for s in (0, 1)
    ]
    lh = []
    for k in range(F):
        cols = at(lax.rem(f + k, F) * RF, RF, 128)
        lh.append(load(h_hbm.at[:, cols], hbuf.at[:, cols]))

    axes = {"dp": (dp, D), "fsdp": (f, F), "ctx": (ctx, C)}

    def peer(axis, k):
        me, n = axes[axis]
        return lax.rem(me + k, n)

    barrier = pltpu.get_barrier_semaphore()
    for axis in axes:
        for k in range(1, axes[axis][1]):
            pl.semaphore_signal(
                barrier, inc=1, device_id={axis: peer(axis, k)},
                device_id_type=pl.DeviceIdType.MESH,
            )

    sent = []

    def send(src, dst, axis, target):
        i = len(sent)
        cp = pltpu.make_async_remote_copy(
            src_ref=src, dst_ref=dst, send_sem=send_sem.at[i], recv_sem=recv_sem.at[i],
            device_id={axis: target}, device_id_type=pl.DeviceIdType.MESH,
        )
        cp.start()
        sent.append(cp)
        return cp

    hd = heads[...]
    tile = min(512, SUB)

    def pointer_rows(p, s):
        def body(t, _):
            r = p * PC + s * SUB + t * tile
            pbuf[at(f * RF + r, tile, tile), :] = mm(kbuf[at(r, tile, tile), :], hd).astype(BF)
            return 0
        lax.fori_loop(0, SUB // tile, body, 0)

    def grows(g, p, s):
        return at(g * RF + p * PC + s * SUB, SUB, SUB)

    ysend = {}
    for s in (0, 1):
        lk[s].wait()
        pointer_rows(par, s)
        if s == 0:
            pl.semaphore_wait(barrier, (D - 1) + (F - 1) + (C - 1))
        for k in range(1, F):
            r = grows(f, par, s)
            ysend[s, k] = send(pbuf.at[r], pbuf.at[r], "fsdp", peer("fsdp", k))
    for s in (0, 1):
        lk[2 + s].wait()
        pointer_rows(other, s)

    adapter = mm(up[...], hd).astype(BF)

    def add_rows(start, n):
        def body(t, _):
            c = at(start + t * tile, tile, 128)
            acc[...] += mm(hbuf[:, c], pbuf[at(start + t * tile, tile, tile), :])
            return 0
        lax.fori_loop(0, n // tile, body, 0)

    acc[...] = jnp.zeros_like(acc)
    lowacc[...] = jnp.zeros_like(lowacc)
    lh[0].wait()
    add_rows(f * RF, RF)
    for k in range(1, F):
        lh[k].wait()

    def low_body(t, _):
        c = at(t * 1024, 1024, 128)
        lowacc[...] += mm_t(hbuf[:, c], down_t[:, c])
        return 0
    lax.fori_loop(0, rows_all // 1024, low_body, 0)
    low = lowacc[...].astype(BF)
    acc[...] += ADAPTER_SCALE * mm(low, adapter)

    def to_column(row):
        return jnp.broadcast_to(row, (128, count)).T

    def segment_of(p):
        end = jnp.zeros((1, 1), jnp.int32)
        total = jnp.zeros(p.shape, F32)
        for n in range(lengths.shape[1] - 1):
            end = end + lengths[:, n : n + 1]
            total = total + jnp.where(p >= end, 1.0, 0.0)
        return total

    seg_row = segment_of(pos[...])
    seg_col[...] = to_column(segment_of(pos[:, at(ctx * count, count, 128)]))
    succ_col[...] = to_column(succ[...].astype(F32))

    relayed = {}
    for s in (0, 1):
        for k in range(1, F):
            g = peer("fsdp", F - k)
            ysend[s, k].wait_recv()
            r = grows(g, par, s)
            relayed[s, k] = send(pbuf.at[r], pbuf.at[r], "dp", mate)
            add_rows(g * RF + par * PC + s * SUB, SUB)
    for s in (0, 1):
        for k in range(1, F):
            relayed[s, k].wait_recv()
            add_rows(peer("fsdp", F - k) * RF + other * PC + s * SUB, SUB)

    rounded = acc[...].astype(BF)
    bl[...] = rounded
    blt[...] = rounded.astype(F32).T.astype(BF)
    keys_t[ctx] = blt[width:, :]
    kcp = [
        send(keys_t.at[ctx], keys_t.at[ctx], "ctx", peer("ctx", k)) for k in range(1, C)
    ]
    for cp in kcp:
        cp.wait_recv()

    scale = 1.0 / math.sqrt(width)
    block = 64
    column = lax.broadcasted_iota(jnp.int32, (1, C * count), 1).astype(F32)

    def soft(t, loss):
        r = at(t * block, block, block)
        q = bl[r, :width]
        sc = jnp.concatenate([mm(q, keys_t[j]) for j in range(C)], axis=1) * scale
        masked = jnp.where(seg_col[r, 0:1] == seg_row, sc, -jnp.inf)
        top = jnp.max(masked, axis=1, keepdims=True)
        e = jnp.exp(masked - top)
        total = jnp.sum(e, axis=1, keepdims=True)
        hit = succ_col[r, 0:1] == column
        picked = jnp.sum(jnp.where(hit, sc, 0.0), axis=1, keepdims=True)
        ws = scale / seqs_all
        wts[r, :] = (e * (ws / total) - jnp.where(hit, ws, 0.0)).astype(BF)
        return loss + (top + jnp.log(total) - picked)

    loss = lax.fori_loop(0, count // block, soft, jnp.zeros((block, 1), F32))
    loss = jnp.sum(loss, axis=0, keepdims=True)

    q_t = blt[:width, :]
    gcp = []
    for k in range(1, C):
        c = at(peer("ctx", k) * count, count, 128)
        gks[k - 1] = mm(q_t, wts[:, c]).astype(BF)
        gcp.append(send(gks.at[k - 1], gkr.at[k - 1], "ctx", peer("ctx", k)))
    gq = mm_t(keys_t[0], wts[:, :count])
    for j in range(1, C):
        gq = gq + mm_t(keys_t[j], wts[:, j * count : (j + 1) * count])
    g_t[0] = gq.astype(BF)
    gk = mm(q_t, wts[:, at(ctx * count, count, 128)])

    ct = min(512, PC)

    def half_start(h):
        g = g_t[h]
        cps = []
        for k in list(range(1, F)) + [0]:
            base = peer("fsdp", k) * RF
            for t in range(PC // ct):
                core_s[h, k, :, t * ct : (t + 1) * ct] = mm(
                    g, hbuf[:, at(base + other * PC + t * ct, ct, 128)]
                ).astype(BF)
            cps.append((k, send(core_s.at[h, k], core_r.at[h, k], "dp", mate)))
        for k in range(F):
            base = peer("fsdp", k) * RF
            for t in range(PC // ct):
                own[h, k, :, t * ct : (t + 1) * ct] = mm(
                    g, hbuf[:, at(base + par * PC + t * ct, ct, 128)]
                )
        ys = []
        for k, cp in cps:
            cp.wait_recv()
            summed = own[h, k] + core_r[h, k].astype(F32)
            if k:
                y_s[h, k - 1] = summed.astype(BF)
                ys.append(
                    (k, send(y_s.at[h, k - 1], y_r.at[h, k - 1], "fsdp", peer("fsdp", k)))
                )
            else:
                own[h, 0] = summed
        return ys

    def half_end(h, ys):
        total = own[h, 0]
        for k, cp in ys:
            cp.wait_recv()
            total = total + y_r[h, k - 1].astype(F32)
        proj[h * width : (h + 1) * width, :] = total.astype(BF)

    yq = half_start(0)
    for k in range(1, C):
        gcp[k - 1].wait_recv()
        gk = gk + gkr[k - 1].astype(F32)
    g_t[1] = gk.astype(BF)
    yk = half_start(1)
    low_t = low.astype(F32).T.astype(BF)
    lg = jnp.concatenate([mm_t(low_t, g_t[0]), mm_t(low_t, g_t[1])], axis=1)
    half_end(0, yq)
    half_end(1, yk)

    piece = pay.shape[0] // D
    part = piece // C
    kw = kbuf.shape[1]
    pr = proj[...]
    for b in range(kw // 256):
        out = mm(pr, kbuf[at(par * PC, PC, PC), b * 256 : (b + 1) * 256])
        pay[b * 256 : b * 256 + 128, :] = out[:, :128].astype(BF)
        pay[b * 256 + 128 : b * 256 + 256, :] = out[:, 128:].astype(BF)
    pay[kw : kw + rank, :] = lg.astype(BF)
    l0 = jnp.broadcast_to(loss, (16, 128))
    hi = l0.astype(BF)
    pay[kw + rank : kw + rank + 16, :] = hi
    pay[kw + rank + 16 : kw + rank + 32, :] = (l0 - hi.astype(F32)).astype(BF)
    pay[kw + rank + 32 :, :] = jnp.zeros((pay.shape[0] - kw - rank - 32, 128), BF)
    c1 = [
        send(pay.at[at(peer("dp", k) * piece, piece, 16)], r1.at[k - 1], "dp", peer("dp", k))
        for k in range(1, D)
    ]
    gdv = ADAPTER_SCALE * mm(adapter, pr)
    pw = PC // C
    for j in range(C):
        gd[j] = gdv[:, j * pw : (j + 1) * pw].astype(BF)
    cg = [(k, send(gd, gd_x.at[k // 2 - 1], "dp", peer("dp", k))) for k in range(2, D, 2)]

    lo = kw + rank

    def add_all(total, refs):
        for ref in refs:
            total = total + ref.astype(F32)
        return total

    for cp in c1:
        cp.wait_recv()
    p2[...] = add_all(
        pay[at(dp * piece, piece, 16), :].astype(F32), [r1[k] for k in range(D - 1)]
    ).astype(p2.dtype)
    c2 = [
        send(p2.at[at(peer("ctx", k) * part, part, 16)], r2.at[k - 1], "ctx", peer("ctx", k))
        for k in range(1, C)
    ]
    for _, cp in cg:
        cp.wait_recv()
    gd2[...] = add_all(gd[...].astype(F32), [gd_x[k // 2 - 1] for k, _ in cg]).astype(BF)
    cg2 = [
        send(gd2.at[peer("ctx", k)], gd_r.at[k - 1], "ctx", peer("ctx", k)) for k in range(1, C)
    ]
    for cp in c2:
        cp.wait_recv()
    r3[f] = add_all(
        p2[at(ctx * part, part, 16), :].astype(F32), [r2[k] for k in range(C - 1)]
    ).astype(r3.dtype)
    c3 = [send(r3.at[f], r3.at[f], "fsdp", peer("fsdp", k)) for k in range(1, F)]
    for cp in cg2:
        cp.wait_recv()
    gd_all[par, ctx] = add_all(gd2[ctx].astype(F32), [gd_r[k] for k in range(C - 1)]).astype(BF)
    cg3 = [
        send(gd_all.at[par, ctx], gd_all.at[par, ctx], "ctx", peer("ctx", k))
        for k in range(1, C)
    ]
    for cp in c3:
        cp.wait_recv()
    mine = at(dp * piece + ctx * part, part, 16)
    fin[mine, :] = add_all(jnp.zeros((part, 128), F32), [r3[k] for k in range(F)]).astype(fin.dtype)
    c4 = [send(fin.at[mine], fin.at[mine], "ctx", peer("ctx", k)) for k in range(1, C)]
    for cp in cg3:
        cp.wait_recv()
    cg4 = send(gd_all.at[par], gd_all.at[par], "dp", mate)
    for cp in c4:
        cp.wait_recv()
    mine = at(dp * piece, piece, 16)
    c5 = [send(fin.at[mine], fin.at[mine], "dp", peer("dp", k)) for k in range(1, D)]
    cg4.wait_recv()
    o_down[...] = gd_all[...].astype(F32)
    for cp in c5:
        cp.wait_recv()

    low_grad = fin[kw : kw + rank, :].astype(BF)
    o_up[...] = ADAPTER_SCALE * mm_t(low_grad, hd)
    lg_t = low_grad.astype(F32).T.astype(BF)
    for b in range(kw // 128):
        up_b = mm(lg_t, up[:, b * 128 : (b + 1) * 128])
        o_grad[b * 128 : (b + 1) * 128, :] = (
            fin[b * 128 : (b + 1) * 128, :].astype(F32) + ADAPTER_SCALE * up_b
        ).T
    o_loss[...] = (
        fin[lo : lo + 8, :].astype(F32) + fin[lo + 16 : lo + 24, :].astype(F32)
    ) * (1.0 / (seqs_all * count * C))
    for cp in sent:
        cp.wait_send()


def on_device(
    box_hidden_states,
    box_token_positions,
    document_lengths,
    successors,
    fixed_key_matrix,
    adapter_down,
    adapter_up,
    pointer_query_map,
    pointer_key_map,
):
    D, F, C = lax.axis_size("dp"), lax.axis_size("fsdp"), lax.axis_size("ctx")
    h = box_hidden_states[0]
    count, rows_all = h.shape
    RF = fixed_key_matrix.shape[0]
    PC = RF // 2
    kw = fixed_key_matrix.shape[1]
    width = pointer_query_map.shape[1]
    rank = adapter_up.shape[0]
    heads = jnp.concatenate([pointer_query_map, pointer_key_map], axis=1)
    unit = D * C * 16
    total = -(-(kw + rank + 32) // unit) * unit
    piece = total // D
    part = piece // C
    V = pltpu.VMEM
    n_sent = (
        2 * (F - 1) * 2 + 2 * (C - 1) + 2 * (F + F - 1) + (D - 1) + (D // 2 - 1)
        + 2 * (C - 1) + (F - 1) + 2 * (C - 1) + 1 + (D - 1)
    )
    vm = pl.BlockSpec(memory_space=pltpu.VMEM)
    hbm = pl.BlockSpec(memory_space=pl.ANY)
    grad, up_grad, down_g, loss = pl.pallas_call(
        functools.partial(kernel, D, F, C, D * F),
        out_shape=(
            jax.ShapeDtypeStruct((kw, 2 * width), F32),
            jax.ShapeDtypeStruct((rank, kw), F32),
            jax.ShapeDtypeStruct((2, C, rank, PC // C), F32),
            jax.ShapeDtypeStruct((8, 128), F32),
        ),
        in_specs=[hbm, hbm] + [vm] * 6,
        out_specs=(vm, vm, vm, vm),
        scratch_shapes=[
            V((count, rows_all), BF),
            V((RF, kw), BF),
            V((rows_all, 2 * width), BF),
            V((count, 2 * width), F32),
            V((count, rank), F32),
            V((count, 2 * width), BF),
            V((2 * width, count), BF),
            V((C, width, count), BF),
            V((count, C * count), BF),
            V((count, 128), F32),
            V((count, 128), F32),
            V((C - 1, width, count), BF),
            V((C - 1, width, count), BF),
            V((2, width, count), BF),
            V((2, F, width, PC), BF),
            V((2, F, width, PC), BF),
            V((2, F, width, PC), F32),
            V((2, F - 1, width, PC), BF),
            V((2, F - 1, width, PC), BF),
            V((2 * width, PC), BF),
            V((total, 128), BF),
            V((D - 1, piece, 128), BF),
            V((piece, 128), BF),
            V((C - 1, part, 128), BF),
            V((part, 128), BF),
            V((F, part, 128), BF),
            V((total, 128), BF),
            V((C, rank, PC // C), BF),
            V((max(D // 2 - 1, 1), C, rank, PC // C), BF),
            V((C, rank, PC // C), BF),
            V((C - 1, rank, PC // C), BF),
            V((2, C, rank, PC // C), BF),
            pltpu.SemaphoreType.DMA((4 + F,)),
            pltpu.SemaphoreType.DMA((n_sent,)),
            pltpu.SemaphoreType.DMA((n_sent,)),
        ],
        compiler_params=pltpu.CompilerParams(
            collective_id=0, has_side_effects=True, vmem_limit_bytes=56 * 1024 * 1024
        ),
    )(
        h, fixed_key_matrix, adapter_down.T, adapter_up, heads,
        box_token_positions, document_lengths, successors,
    )
    return (
        down_g.transpose(0, 1, 3, 2).reshape(RF, rank),
        up_grad,
        grad[:, :width],
        grad[:, width:],
        loss[0, 0],
    )


def solution(mesh):
    in_specs = (
        P(("dp", "fsdp"), "ctx", None),
        P(("dp", "fsdp"), None),
        P(("dp", "fsdp"), None),
        P(("dp", "fsdp"), "ctx"),
        P("fsdp", None),
        P(),
        P(),
        P(),
        P(),
    )
    out_specs = (P("fsdp", None), P(), P(), P(), P())
    return jax.shard_map(
        on_device, mesh=mesh, in_specs=in_specs, out_specs=out_specs, check_vma=False
    )
```

```python
import functools
import math

import jax
import jax.numpy as jnp
from jax import lax
from jax.experimental import pallas as pl
from jax.experimental.pallas import tpu as pltpu
from jax.sharding import PartitionSpec as P

ADAPTER_SCALE = 0.5
BF = jnp.bfloat16
F32 = jnp.float32


def mm(a, b):
    return lax.dot_general(a, b, (((1,), (0,)), ((), ())), preferred_element_type=F32)


def mm_t(a, b):
    return lax.dot_general(a, b, (((1,), (1,)), ((), ())), preferred_element_type=F32)


def at(start, size, unit):
    return pl.ds(pl.multiple_of(start, unit), size)


def kernel(
    D, F, C, seqs_all,
    h_hbm, k_hbm, down_t, up, qmap_t, kmap_t, pos, lengths, succ,
    fin, gd_all,
    hd, hbuf, kbuf, pbuf, acc, lowacc, bl, blt, keys_t, wts, seg_col, succ_col,
    gks, gkr, g_t, core_s, core_r, own, y_s, y_r, proj,
    pay, r1, p2, r2, r3, gd, gd_x, gd2, gd_r,
    load_sem, send_sem, recv_sem,
):
    rows_all, rank = hbuf.shape[1], up.shape[0]
    count, width = hbuf.shape[0], bl.shape[1] // 2
    RF = rows_all // F
    PC = RF // 2
    NS = min(4, PC // 256)
    SUB = PC // (2 * NS)
    dp, f, ctx = lax.axis_index("dp"), lax.axis_index("fsdp"), lax.axis_index("ctx")
    par = lax.rem(dp, 2)
    mate = dp + 1 - 2 * par
    other = 1 - par
    near = (dp // 2) * NS * SUB
    far = NS * SUB - near
    across = lax.rem(dp + D // 2, D)

    loads = []

    def load(src, dst):
        cp = pltpu.make_async_copy(src, dst, load_sem.at[len(loads)])
        cp.start()
        loads.append(cp)
        return cp

    def load_rows(start, n):
        r = at(start, n, SUB)
        return load(k_hbm.at[r], kbuf.at[r])

    lk = [load_rows(par * PC + near, NS * SUB), load_rows(par * PC + far, NS * SUB)]
    lk.append(load_rows(other * PC, PC))
    lh = []
    for k in range(F):
        cols = at(lax.rem(f + k, F) * RF, RF, 128)
        lh.append(load(h_hbm.at[:, cols], hbuf.at[:, cols]))

    axes = {"dp": (dp, D), "fsdp": (f, F), "ctx": (ctx, C)}

    def peer(axis, k):
        me, n = axes[axis]
        return lax.rem(me + k, n)

    barrier = pltpu.get_barrier_semaphore()
    for axis in axes:
        for k in range(1, axes[axis][1]):
            pl.semaphore_signal(
                barrier, inc=1, device_id={axis: peer(axis, k)},
                device_id_type=pl.DeviceIdType.MESH,
            )

    sent = []

    def send(src, dst, axis, target):
        i = len(sent)
        cp = pltpu.make_async_remote_copy(
            src_ref=src, dst_ref=dst, send_sem=send_sem.at[i], recv_sem=recv_sem.at[i],
            device_id={axis: target}, device_id_type=pl.DeviceIdType.MESH,
        )
        cp.start()
        sent.append(cp)
        return cp

    hd_t = jnp.concatenate([qmap_t[...], kmap_t[...]], axis=0)
    hd[...] = hd_t.astype(F32).T.astype(BF)

    def pointer_rows(start, n):
        tile = min(512, n)

        def body(t, _):
            r = start + t * tile
            pbuf[at(f * RF + r, tile, 64), :] = mm(kbuf[at(r, tile, 64), :], hd[...]).astype(BF)
            return 0
        lax.fori_loop(0, n // tile, body, 0)

    def grows(g, p, part_of, s):
        return at(g * RF + p * PC + part_of + s * SUB, SUB, SUB)

    ysend = {}
    lk[0].wait()
    pointer_rows(par * PC + near, NS * SUB)
    pl.semaphore_wait(barrier, (D - 1) + (F - 1) + (C - 1))
    for s in range(NS):
        for k in range(1, F):
            r = grows(f, par, near, s)
            ysend[s, k] = send(pbuf.at[r], pbuf.at[r], "fsdp", peer("fsdp", k))
    lk[1].wait()
    pointer_rows(par * PC + far, NS * SUB)
    lk[2].wait()
    pointer_rows(other * PC, PC)

    adapter = mm(up[...], hd[...]).astype(BF)

    def add_rows(start, n):
        tile = min(1024, n)

        def body(t, _):
            c = at(start + t * tile, tile, 128)
            acc[...] += mm(hbuf[:, c], pbuf[at(start + t * tile, tile, 128), :])
            return 0
        lax.fori_loop(0, n // tile, body, 0)

    acc[...] = jnp.zeros_like(acc)
    lowacc[...] = jnp.zeros_like(lowacc)
    for k in range(F):
        lh[k].wait()

    def to_column(row):
        return jnp.broadcast_to(row, (128, count)).T

    def segment_of(p):
        end = jnp.zeros((1, 1), jnp.int32)
        total = jnp.zeros(p.shape, F32)
        for n in range(lengths.shape[1] - 1):
            end = end + lengths[:, n : n + 1]
            total = total + jnp.where(p >= end, 1.0, 0.0)
        return total

    seg_row = segment_of(pos[...])
    seg_col[...] = to_column(segment_of(pos[:, at(ctx * count, count, 128)]))
    succ_col[...] = to_column(succ[...].astype(F32))

    low_tile = rows_all // NS
    xsend, relay_y, relay_x = {}, {}, {}

    def take_x(s):
        for k in range(1, F):
            g = peer("fsdp", F - k)
            xsend[s, k].wait_recv()
            r = grows(g, par, far, s)
            relay_x[s, k] = send(pbuf.at[r], pbuf.at[r], "dp", mate)

    for s in range(NS):
        for k in range(1, F):
            g = peer("fsdp", F - k)
            ysend[s, k].wait_recv()
            r = grows(g, par, near, s)
            xsend[s, k] = send(pbuf.at[r], pbuf.at[r], "dp", across)
            relay_y[s, k] = send(pbuf.at[r], pbuf.at[r], "dp", mate)
        add_rows(f * RF + s * (RF // NS), RF // NS)
        if s:
            take_x(s - 1)
        c = slice(s * low_tile, (s + 1) * low_tile)
        lowacc[...] += mm_t(hbuf[:, c], down_t[:, c])
    low = lowacc[...].astype(BF)
    acc[...] += ADAPTER_SCALE * mm(low, adapter)
    take_x(NS - 1)
    for k in range(1, F):
        base = peer("fsdp", F - k) * RF
        add_rows(base + par * PC, PC)
        for s in range(NS):
            relay_y[s, k].wait_recv()
        add_rows(base + other * PC + near, NS * SUB)
        for s in range(NS):
            relay_x[s, k].wait_recv()
        add_rows(base + other * PC + far, NS * SUB)

    rounded = acc[...].astype(BF)
    bl[...] = rounded
    blt[...] = rounded.astype(F32).T.astype(BF)
    keys_t[ctx] = blt[width:, :]
    kcp = [
        send(keys_t.at[ctx], keys_t.at[ctx], "ctx", peer("ctx", k)) for k in range(1, C)
    ]
    for cp in kcp:
        cp.wait_recv()

    scale = 1.0 / math.sqrt(width)
    block = 64
    column = lax.broadcasted_iota(jnp.int32, (1, C * count), 1).astype(F32)

    def soft(t, loss):
        r = at(t * block, block, block)
        q = bl[r, :width]
        sc = jnp.concatenate([mm(q, keys_t[j]) for j in range(C)], axis=1) * scale
        masked = jnp.where(seg_col[r, 0:1] == seg_row, sc, -jnp.inf)
        top = jnp.max(masked, axis=1, keepdims=True)
        e = jnp.exp(masked - top)
        total = jnp.sum(e, axis=1, keepdims=True)
        hit = succ_col[r, 0:1] == column
        picked = jnp.sum(jnp.where(hit, sc, 0.0), axis=1, keepdims=True)
        ws = scale / seqs_all
        wts[r, :] = (e * (ws / total) - jnp.where(hit, ws, 0.0)).astype(BF)
        return loss + (top + jnp.log(total) - picked)

    loss = lax.fori_loop(0, count // block, soft, jnp.zeros((block, 1), F32))
    loss = jnp.sum(loss, axis=0, keepdims=True)

    q_t = blt[:width, :]
    gcp = []
    for k in range(1, C):
        c = at(peer("ctx", k) * count, count, 128)
        gks[k - 1] = mm(q_t, wts[:, c]).astype(BF)
        gcp.append(send(gks.at[k - 1], gkr.at[k - 1], "ctx", peer("ctx", k)))
    gq = mm_t(keys_t[0], wts[:, :count])
    for j in range(1, C):
        gq = gq + mm_t(keys_t[j], wts[:, j * count : (j + 1) * count])
    g_t[0] = gq.astype(BF)
    gk = mm(q_t, wts[:, at(ctx * count, count, 128)])

    ct = min(512, PC)

    def half_start(h):
        g = g_t[h]
        cps = []
        for k in list(range(1, F)) + [0]:
            base = peer("fsdp", k) * RF
            for t in range(PC // ct):
                core_s[h, k, :, t * ct : (t + 1) * ct] = mm(
                    g, hbuf[:, at(base + other * PC + t * ct, ct, 128)]
                ).astype(BF)
            cps.append((k, send(core_s.at[h, k], core_r.at[h, k], "dp", mate)))
        for k in range(F):
            base = peer("fsdp", k) * RF
            for t in range(PC // ct):
                own[h, k, :, t * ct : (t + 1) * ct] = mm(
                    g, hbuf[:, at(base + par * PC + t * ct, ct, 128)]
                )
        ys = []
        for k, cp in cps:
            cp.wait_recv()
            summed = own[h, k] + core_r[h, k].astype(F32)
            if k:
                y_s[h, k - 1] = summed.astype(BF)
                ys.append(
                    (k, send(y_s.at[h, k - 1], y_r.at[h, k - 1], "fsdp", peer("fsdp", k)))
                )
            else:
                own[h, 0] = summed
        return ys

    def half_end(h, ys):
        total = own[h, 0]
        for k, cp in ys:
            cp.wait_recv()
            total = total + y_r[h, k - 1].astype(F32)
        proj[h] = total.astype(BF)

    yq = half_start(0)
    for k in range(1, C):
        gcp[k - 1].wait_recv()
        gk = gk + gkr[k - 1].astype(F32)
    g_t[1] = gk.astype(BF)
    yk = half_start(1)
    low_t = low.astype(F32).T.astype(BF)
    lg = jnp.concatenate([mm_t(low_t, g_t[0]), mm_t(low_t, g_t[1])], axis=1)
    def add_all(total, refs):
        for ref in refs:
            total = total + ref.astype(F32)
        return total

    kw = kbuf.shape[1]
    body_rows = kw // 128 * width
    offset = (0, body_rows)
    sizes = (body_rows, pay.shape[0] - body_rows)

    def share(h):
        base = offset[h]
        pr = proj[h]
        for b in range(kw // 256):
            out = mm(pr, kbuf[at(par * PC, PC, 128), b * 256 : (b + 1) * 256])
            for u in (0, 1):
                r = base + (2 * b + u) * width
                pay[r : r + width, :] = out[:, u * 128 : (u + 1) * 128].astype(BF)
        if h:
            r = base + body_rows
            pay[r : r + rank, :] = lg.astype(BF)
            l0 = jnp.broadcast_to(loss, (16, 128))
            hi = l0.astype(BF)
            pay[r + rank : r + rank + 16, :] = hi
            pay[r + rank + 16 : r + rank + 32, :] = (l0 - hi.astype(F32)).astype(BF)
            r = r + rank + 32
            pay[r:, :] = jnp.zeros((pay.shape[0] - r, 128), BF)
        n = sizes[h] // D
        return [
            send(
                pay.at[at(base + peer("dp", k) * n, n, 16)], r1.at[h, k - 1, 0:n],
                "dp", peer("dp", k),
            )
            for k in range(1, D)
        ]

    def wait_all(cps):
        for cp in cps:
            cp.wait_recv()

    def over_ctx(h, cps):
        n = sizes[h] // D
        m = n // C
        wait_all(cps)
        p2[h, 0:n] = add_all(
            pay[at(offset[h] + dp * n, n, 16), :].astype(F32),
            [r1[h, k, 0:n] for k in range(D - 1)],
        ).astype(BF)
        return [
            send(
                p2.at[h, at(peer("ctx", k) * m, m, 16)], r2.at[h, k - 1, 0:m],
                "ctx", peer("ctx", k),
            )
            for k in range(1, C)
        ]

    def over_fsdp(h, cps):
        m = sizes[h] // D // C
        wait_all(cps)
        r3[h, f, 0:m] = add_all(
            p2[h, at(ctx * m, m, 16), :].astype(F32), [r2[h, k, 0:m] for k in range(C - 1)]
        ).astype(BF)
        mine = r3.at[h, f, 0:m]
        return [send(mine, mine, "fsdp", peer("fsdp", k)) for k in range(1, F)]

    def back_ctx(h, cps):
        n = sizes[h] // D
        m = n // C
        wait_all(cps)
        mine = at(offset[h] + dp * n + ctx * m, m, 16)
        fin[mine, :] = add_all(
            jnp.zeros((m, 128), F32), [r3[h, k, 0:m] for k in range(F)]
        ).astype(BF)
        return [send(fin.at[mine], fin.at[mine], "ctx", peer("ctx", k)) for k in range(1, C)]

    def back_dp(h, cps):
        n = sizes[h] // D
        wait_all(cps)
        mine = at(offset[h] + dp * n, n, 16)
        return [send(fin.at[mine], fin.at[mine], "dp", peer("dp", k)) for k in range(1, D)]

    half_end(0, yq)
    a0 = over_ctx(0, share(0))
    half_end(1, yk)
    a1 = share(1)
    gdv = ADAPTER_SCALE * (mm(adapter[:, :width], proj[0]) + mm(adapter[:, width:], proj[1]))
    pw = PC // C
    for j in range(C):
        gd[j] = gdv[:, j * pw : (j + 1) * pw].astype(BF)
    cg = [(k, send(gd, gd_x.at[k // 2 - 1], "dp", peer("dp", k))) for k in range(2, D, 2)]
    a0 = over_fsdp(0, a0)
    a1 = over_ctx(1, a1)
    a0 = back_ctx(0, a0)
    wait_all([cp for _, cp in cg])
    gd2[...] = add_all(gd[...].astype(F32), [gd_x[k // 2 - 1] for k, _ in cg]).astype(BF)
    cg2 = [
        send(gd2.at[peer("ctx", k)], gd_r.at[k - 1], "ctx", peer("ctx", k)) for k in range(1, C)
    ]
    a1 = over_fsdp(1, a1)
    a0 = back_dp(0, a0)
    wait_all(cg2)
    gd_all[par, ctx] = add_all(gd2[ctx].astype(F32), [gd_r[k] for k in range(C - 1)]).astype(BF)
    cg3 = [
        send(gd_all.at[par, ctx], gd_all.at[par, ctx], "ctx", peer("ctx", k))
        for k in range(1, C)
    ]
    a1 = back_ctx(1, a1)
    wait_all(cg3)
    cg4 = send(gd_all.at[par], gd_all.at[par], "dp", mate)
    a1 = back_dp(1, a1)
    wait_all(a0)
    wait_all(a1)
    cg4.wait_recv()
    for cp in sent:
        cp.wait_send()


def outputs(scale, fin, gd_all, up, qmap_t, kmap_t, o_q, o_k, o_up, o_down, o_loss):
    rank, kw = up.shape
    width = o_q.shape[0]
    body_rows = kw // 128 * width
    r = 2 * body_rows
    low_grad = fin[r : r + rank, :]
    hd_t = jnp.concatenate([qmap_t[...], kmap_t[...]], axis=0)
    o_up[...] = ADAPTER_SCALE * mm(low_grad, hd_t)
    lg_t = low_grad.astype(F32).T.astype(BF)
    upper = ADAPTER_SCALE * mm(lg_t, up[...])
    for h, o in ((0, o_q), (1, o_k)):
        for b in range(kw // 128):
            r0 = h * body_rows + b * width
            c = slice(b * 128, (b + 1) * 128)
            o[:, c] = fin[r0 : r0 + width, :].astype(F32) + upper[h * width : (h + 1) * width, c]
    halves, C, _, pw = gd_all.shape
    for p in range(halves):
        for j in range(C):
            at0 = (p * C + j) * pw
            o_down[:, at0 : at0 + pw] = gd_all[p, j].astype(F32)
    l0 = r + rank
    both = fin[l0 : l0 + 16, :].astype(F32) + fin[l0 + 16 : l0 + 32, :].astype(F32)
    o_loss[...] = both[0:1, 0:1] * scale


def on_device(
    box_hidden_states,
    box_token_positions,
    document_lengths,
    successors,
    fixed_key_matrix,
    adapter_down,
    adapter_up,
    pointer_query_map,
    pointer_key_map,
):
    D, F, C = lax.axis_size("dp"), lax.axis_size("fsdp"), lax.axis_size("ctx")
    h = box_hidden_states[0]
    count, rows_all = h.shape
    RF = fixed_key_matrix.shape[0]
    PC = RF // 2
    kw = fixed_key_matrix.shape[1]
    width = pointer_query_map.shape[1]
    rank = adapter_up.shape[0]
    unit = D * C * 16
    first = kw // 128 * width
    second = -(-(first + rank + 32) // unit) * unit
    total = first + second
    piece = second // D
    part = piece // C
    NS = min(4, PC // 256)
    V = pltpu.VMEM
    n_sent = (
        4 * NS * (F - 1) + 2 * (C - 1) + 2 * (F + F - 1) + (D // 2 - 1) + 2 * (C - 1) + 1
        + 2 * (2 * (D - 1) + 2 * (C - 1) + (F - 1))
    )
    vm = pl.BlockSpec(memory_space=pltpu.VMEM)
    hbm = pl.BlockSpec(memory_space=pl.ANY)
    qmap_t, kmap_t = pointer_query_map.T, pointer_key_map.T
    fin, gd_all = pl.pallas_call(
        functools.partial(kernel, D, F, C, D * F),
        out_shape=(
            jax.ShapeDtypeStruct((total, 128), BF),
            jax.ShapeDtypeStruct((2, C, rank, PC // C), BF),
        ),
        in_specs=[hbm, hbm] + [vm] * 7,
        out_specs=(vm, vm),
        scratch_shapes=[
            V((kw, 2 * width), BF),
            V((count, rows_all), BF),
            V((RF, kw), BF),
            V((rows_all, 2 * width), BF),
            V((count, 2 * width), F32),
            V((count, rank), F32),
            V((count, 2 * width), BF),
            V((2 * width, count), BF),
            V((C, width, count), BF),
            V((count, C * count), BF),
            V((count, 128), F32),
            V((count, 128), F32),
            V((C - 1, width, count), BF),
            V((C - 1, width, count), BF),
            V((2, width, count), BF),
            V((2, F, width, PC), BF),
            V((2, F, width, PC), BF),
            V((2, F, width, PC), F32),
            V((2, F - 1, width, PC), BF),
            V((2, F - 1, width, PC), BF),
            V((2, width, PC), BF),
            V((total, 128), BF),
            V((2, D - 1, piece, 128), BF),
            V((2, piece, 128), BF),
            V((2, C - 1, part, 128), BF),
            V((2, F, part, 128), BF),
            V((C, rank, PC // C), BF),
            V((max(D // 2 - 1, 1), C, rank, PC // C), BF),
            V((C, rank, PC // C), BF),
            V((C - 1, rank, PC // C), BF),
            pltpu.SemaphoreType.DMA((3 + F,)),
            pltpu.SemaphoreType.DMA((n_sent,)),
            pltpu.SemaphoreType.DMA((n_sent,)),
        ],
        compiler_params=pltpu.CompilerParams(
            collective_id=0, has_side_effects=True, vmem_limit_bytes=56 * 1024 * 1024
        ),
    )(
        h, fixed_key_matrix, adapter_down.T, adapter_up, qmap_t, kmap_t,
        box_token_positions, document_lengths, successors,
    )
    grad_q, grad_k, up_grad, down_t, loss = pl.pallas_call(
        functools.partial(outputs, 1.0 / (D * F * count * C)),
        out_shape=(
            jax.ShapeDtypeStruct((width, kw), F32),
            jax.ShapeDtypeStruct((width, kw), F32),
            jax.ShapeDtypeStruct((rank, kw), F32),
            jax.ShapeDtypeStruct((rank, RF), F32),
            jax.ShapeDtypeStruct((1, 1), F32),
        ),
        in_specs=[vm] * 5,
        out_specs=(vm,) * 5,
    )(fin, gd_all, adapter_up, qmap_t, kmap_t)
    return down_t.T, up_grad, grad_q.T, grad_k.T, loss[0, 0]


def solution(mesh):
    in_specs = (
        P(("dp", "fsdp"), "ctx", None),
        P(("dp", "fsdp"), None),
        P(("dp", "fsdp"), None),
        P(("dp", "fsdp"), "ctx"),
        P("fsdp", None),
        P(),
        P(),
        P(),
        P(),
    )
    out_specs = (P("fsdp", None), P(), P(), P(), P())
    return jax.shard_map(
        on_device, mesh=mesh, in_specs=in_specs, out_specs=out_specs, check_vma=False
    )
```

```python
import functools
import math

import jax
import jax.numpy as jnp
from jax import lax
from jax.experimental import pallas as pl
from jax.experimental.pallas import tpu as pltpu
from jax.sharding import PartitionSpec as P

ADAPTER_SCALE = 0.5
BF = jnp.bfloat16
F32 = jnp.float32


def mm(a, b):
    return lax.dot_general(a, b, (((1,), (0,)), ((), ())), preferred_element_type=F32)


def mm_t(a, b):
    return lax.dot_general(a, b, (((1,), (1,)), ((), ())), preferred_element_type=F32)


def at(start, size, unit):
    return pl.ds(pl.multiple_of(start, unit), size)


def kernel(
    D, F, C, seqs_all,
    h_hbm, k_hbm, down_t, up, qmap_t, kmap_t, pos, lengths, succ,
    fin, gd_all,
    hd, hbuf, kbuf, pbuf, acc, lowacc, bl, blt, keys_t, wts, seg_col, succ_col,
    gks, gkr, g_t, core_s, core_r, own, y_s, y_r, proj,
    pay, r1, p2, r2, r3, gd, gd_x, gd2, gd_r,
    load_sem, send_sem, recv_sem,
):
    rows_all, rank = hbuf.shape[1], up.shape[0]
    count, width = hbuf.shape[0], bl.shape[1] // 2
    RF = rows_all // F
    PC = RF // 2
    NS = min(4, PC // 256)
    SUB = PC // (2 * NS)
    dp, f, ctx = lax.axis_index("dp"), lax.axis_index("fsdp"), lax.axis_index("ctx")
    par = lax.rem(dp, 2)
    mate = dp + 1 - 2 * par
    other = 1 - par
    near = (dp // 2) * NS * SUB
    far = NS * SUB - near
    across = lax.rem(dp + D // 2, D)

    loads = []

    def load(src, dst):
        cp = pltpu.make_async_copy(src, dst, load_sem.at[len(loads)])
        cp.start()
        loads.append(cp)
        return cp

    def load_rows(start, n):
        r = at(start, n, SUB)
        return load(k_hbm.at[r], kbuf.at[r])

    lk = [load_rows(par * PC + near, NS * SUB), load_rows(par * PC + far, NS * SUB)]
    lk.append(load_rows(other * PC, PC))
    lh = []
    for k in range(F):
        cols = at(lax.rem(f + k, F) * RF, RF, 128)
        lh.append(load(h_hbm.at[:, cols], hbuf.at[:, cols]))

    axes = {"dp": (dp, D), "fsdp": (f, F), "ctx": (ctx, C)}

    def peer(axis, k):
        me, n = axes[axis]
        return lax.rem(me + k, n)

    barrier = pltpu.get_barrier_semaphore()
    for axis in axes:
        for k in range(1, axes[axis][1]):
            pl.semaphore_signal(
                barrier, inc=1, device_id={axis: peer(axis, k)},
                device_id_type=pl.DeviceIdType.MESH,
            )

    sent = []

    def send(src, dst, axis, target):
        i = len(sent)
        cp = pltpu.make_async_remote_copy(
            src_ref=src, dst_ref=dst, send_sem=send_sem.at[i], recv_sem=recv_sem.at[i],
            device_id={axis: target}, device_id_type=pl.DeviceIdType.MESH,
        )
        cp.start()
        sent.append(cp)
        return cp

    hd_t = jnp.concatenate([qmap_t[...], kmap_t[...]], axis=0)
    hd[...] = hd_t.astype(F32).T.astype(BF)

    def pointer_rows(start, n):
        tile = min(512, n)

        def body(t, _):
            r = start + t * tile
            pbuf[at(f * RF + r, tile, 64), :] = mm(kbuf[at(r, tile, 64), :], hd[...]).astype(BF)
            return 0
        lax.fori_loop(0, n // tile, body, 0)

    def grows(g, p, part_of, s):
        return at(g * RF + p * PC + part_of + s * SUB, SUB, SUB)

    adapter = mm(up[...], hd[...]).astype(BF)

    acc[...] = jnp.zeros_like(acc)
    lowacc[...] = jnp.zeros_like(lowacc)
    def to_column(row):
        return jnp.broadcast_to(row, (128, count)).T

    def segment_of(p):
        end = jnp.zeros((1, 1), jnp.int32)
        total = jnp.zeros(p.shape, F32)
        for n in range(lengths.shape[1] - 1):
            end = end + lengths[:, n : n + 1]
            total = total + jnp.where(p >= end, 1.0, 0.0)
        return total

    seg_row = segment_of(pos[...])
    seg_col[...] = to_column(segment_of(pos[:, at(ctx * count, count, 128)]))
    succ_col[...] = to_column(succ[...].astype(F32))

    ysend = {}
    lk[0].wait()
    pointer_rows(par * PC + near, NS * SUB)
    pl.semaphore_wait(barrier, (D - 1) + (F - 1) + (C - 1))
    for s in range(NS):
        for k in range(1, F):
            r = grows(f, par, near, s)
            ysend[s, k] = send(pbuf.at[r], pbuf.at[r], "fsdp", peer("fsdp", k))
    lk[1].wait()
    pointer_rows(par * PC + far, NS * SUB)
    lk[2].wait()
    pointer_rows(other * PC, PC)

    def add_rows(start, n):
        tile = min(1024, n)

        def body(t, _):
            c = at(start + t * tile, tile, 128)
            acc[...] += mm(hbuf[:, c], pbuf[at(start + t * tile, tile, 128), :])
            return 0
        lax.fori_loop(0, n // tile, body, 0)

    for k in range(F):
        lh[k].wait()

    low_tile = rows_all // NS
    xsend, relay_y, relay_x = {}, {}, {}

    def take_x(s):
        for k in range(1, F):
            g = peer("fsdp", F - k)
            xsend[s, k].wait_recv()
            r = grows(g, par, far, s)
            relay_x[s, k] = send(pbuf.at[r], pbuf.at[r], "dp", mate)

    for s in range(NS):
        for k in range(1, F):
            g = peer("fsdp", F - k)
            ysend[s, k].wait_recv()
            r = grows(g, par, near, s)
            xsend[s, k] = send(pbuf.at[r], pbuf.at[r], "dp", across)
            relay_y[s, k] = send(pbuf.at[r], pbuf.at[r], "dp", mate)
        add_rows(f * RF + s * (RF // NS), RF // NS)
        if s:
            take_x(s - 1)
        c = slice(s * low_tile, (s + 1) * low_tile)
        lowacc[...] += mm_t(hbuf[:, c], down_t[:, c])
    low = lowacc[...].astype(BF)
    acc[...] += ADAPTER_SCALE * mm(low, adapter)
    take_x(NS - 1)
    for k in range(1, F):
        base = peer("fsdp", F - k) * RF
        add_rows(base + par * PC, PC)
        for s in range(NS):
            relay_y[s, k].wait_recv()
        add_rows(base + other * PC + near, NS * SUB)
        for s in range(NS):
            relay_x[s, k].wait_recv()
        add_rows(base + other * PC + far, NS * SUB)

    rounded = acc[...].astype(BF)
    bl[...] = rounded
    blt[...] = rounded.astype(F32).T.astype(BF)
    keys_t[ctx] = blt[width:, :]
    kcp = [
        send(keys_t.at[ctx], keys_t.at[ctx], "ctx", peer("ctx", k)) for k in range(1, C)
    ]
    for cp in kcp:
        cp.wait_recv()

    scale = 1.0 / math.sqrt(width)
    block = 64
    column = lax.broadcasted_iota(jnp.int32, (1, C * count), 1).astype(F32)

    def soft(t, loss):
        r = at(t * block, block, block)
        q = bl[r, :width]
        sc = jnp.concatenate([mm(q, keys_t[j]) for j in range(C)], axis=1) * scale
        masked = jnp.where(seg_col[r, 0:1] == seg_row, sc, -jnp.inf)
        top = jnp.max(masked, axis=1, keepdims=True)
        e = jnp.exp(masked - top)
        total = jnp.sum(e, axis=1, keepdims=True)
        hit = succ_col[r, 0:1] == column
        picked = jnp.sum(jnp.where(hit, sc, 0.0), axis=1, keepdims=True)
        ws = scale / seqs_all
        wts[r, :] = (e * (ws / total) - jnp.where(hit, ws, 0.0)).astype(BF)
        return loss + (top + jnp.log(total) - picked)

    loss = lax.fori_loop(0, count // block, soft, jnp.zeros((block, 1), F32))
    loss = jnp.sum(loss, axis=0, keepdims=True)

    q_t = blt[:width, :]
    gcp = []
    for k in range(1, C):
        c = at(peer("ctx", k) * count, count, 128)
        gks[k - 1] = mm(q_t, wts[:, c]).astype(BF)
        gcp.append(send(gks.at[k - 1], gkr.at[k - 1], "ctx", peer("ctx", k)))
    gq = mm_t(keys_t[0], wts[:, :count])
    for j in range(1, C):
        gq = gq + mm_t(keys_t[j], wts[:, j * count : (j + 1) * count])
    g_t[0] = gq.astype(BF)
    gk = mm(q_t, wts[:, at(ctx * count, count, 128)])

    ct = min(512, PC)

    def half_start(h):
        g = g_t[h]
        cps = []
        for k in list(range(1, F)) + [0]:
            base = peer("fsdp", k) * RF
            for t in range(PC // ct):
                core_s[h, k, :, t * ct : (t + 1) * ct] = mm(
                    g, hbuf[:, at(base + other * PC + t * ct, ct, 128)]
                ).astype(BF)
            cps.append((k, send(core_s.at[h, k], core_r.at[h, k], "dp", mate)))
        for k in range(F):
            base = peer("fsdp", k) * RF
            for t in range(PC // ct):
                own[h, k, :, t * ct : (t + 1) * ct] = mm(
                    g, hbuf[:, at(base + par * PC + t * ct, ct, 128)]
                )
        ys = []
        for k, cp in cps:
            cp.wait_recv()
            summed = own[h, k] + core_r[h, k].astype(F32)
            if k:
                y_s[h, k - 1] = summed.astype(BF)
                ys.append(
                    (k, send(y_s.at[h, k - 1], y_r.at[h, k - 1], "fsdp", peer("fsdp", k)))
                )
            else:
                own[h, 0] = summed
        return ys

    def half_end(h, ys):
        total = own[h, 0]
        for k, cp in ys:
            cp.wait_recv()
            total = total + y_r[h, k - 1].astype(F32)
        proj[h] = total.astype(BF)

    yq = half_start(0)
    for k in range(1, C):
        gcp[k - 1].wait_recv()
        gk = gk + gkr[k - 1].astype(F32)
    g_t[1] = gk.astype(BF)
    yk = half_start(1)
    low_t = low.astype(F32).T.astype(BF)
    lg = jnp.concatenate([mm_t(low_t, g_t[0]), mm_t(low_t, g_t[1])], axis=1)
    def add_all(total, refs):
        for ref in refs:
            total = total + ref.astype(F32)
        return total

    kw = kbuf.shape[1]
    body_rows = kw // 128 * width
    offset = (0, body_rows)
    sizes = (body_rows, pay.shape[0] - body_rows)

    def share(h):
        base = offset[h]
        pr = proj[h]
        for b in range(kw // 256):
            out = mm(pr, kbuf[at(par * PC, PC, 128), b * 256 : (b + 1) * 256])
            for u in (0, 1):
                r = base + (2 * b + u) * width
                pay[r : r + width, :] = out[:, u * 128 : (u + 1) * 128].astype(BF)
        if h:
            r = base + body_rows
            pay[r : r + rank, :] = lg.astype(BF)
            l0 = jnp.broadcast_to(loss, (16, 128))
            hi = l0.astype(BF)
            pay[r + rank : r + rank + 16, :] = hi
            pay[r + rank + 16 : r + rank + 32, :] = (l0 - hi.astype(F32)).astype(BF)
            r = r + rank + 32
            pay[r:, :] = jnp.zeros((pay.shape[0] - r, 128), BF)
        n = sizes[h] // D
        return [
            send(
                pay.at[at(base + peer("dp", k) * n, n, 16)], r1.at[h, k - 1, 0:n],
                "dp", peer("dp", k),
            )
            for k in range(1, D)
        ]

    def wait_all(cps):
        for cp in cps:
            cp.wait_recv()

    def over_ctx(h, cps):
        n = sizes[h] // D
        m = n // C
        wait_all(cps)
        p2[h, 0:n] = add_all(
            pay[at(offset[h] + dp * n, n, 16), :].astype(F32),
            [r1[h, k, 0:n] for k in range(D - 1)],
        ).astype(BF)
        return [
            send(
                p2.at[h, at(peer("ctx", k) * m, m, 16)], r2.at[h, k - 1, 0:m],
                "ctx", peer("ctx", k),
            )
            for k in range(1, C)
        ]

    def over_fsdp(h, cps):
        m = sizes[h] // D // C
        wait_all(cps)
        r3[h, f, 0:m] = add_all(
            p2[h, at(ctx * m, m, 16), :].astype(F32), [r2[h, k, 0:m] for k in range(C - 1)]
        ).astype(BF)
        mine = r3.at[h, f, 0:m]
        return [send(mine, mine, "fsdp", peer("fsdp", k)) for k in range(1, F)]

    def back_ctx(h, cps):
        n = sizes[h] // D
        m = n // C
        wait_all(cps)
        mine = at(offset[h] + dp * n + ctx * m, m, 16)
        fin[mine, :] = add_all(
            jnp.zeros((m, 128), F32), [r3[h, k, 0:m] for k in range(F)]
        ).astype(BF)
        return [send(fin.at[mine], fin.at[mine], "ctx", peer("ctx", k)) for k in range(1, C)]

    def back_dp(h, cps):
        n = sizes[h] // D
        wait_all(cps)
        mine = at(offset[h] + dp * n, n, 16)
        return [send(fin.at[mine], fin.at[mine], "dp", peer("dp", k)) for k in range(1, D)]

    half_end(0, yq)
    a0 = over_ctx(0, share(0))
    half_end(1, yk)
    a1 = share(1)
    gdv = ADAPTER_SCALE * (mm(adapter[:, :width], proj[0]) + mm(adapter[:, width:], proj[1]))
    pw = PC // C
    for j in range(C):
        gd[j] = gdv[:, j * pw : (j + 1) * pw].astype(BF)
    cg = [(k, send(gd, gd_x.at[k // 2 - 1], "dp", peer("dp", k))) for k in range(2, D, 2)]
    a0 = over_fsdp(0, a0)
    a1 = over_ctx(1, a1)
    a0 = back_ctx(0, a0)
    wait_all([cp for _, cp in cg])
    gd2[...] = add_all(gd[...].astype(F32), [gd_x[k // 2 - 1] for k, _ in cg]).astype(BF)
    cg2 = [
        send(gd2.at[peer("ctx", k)], gd_r.at[k - 1], "ctx", peer("ctx", k)) for k in range(1, C)
    ]
    a1 = over_fsdp(1, a1)
    a0 = back_dp(0, a0)
    wait_all(cg2)
    gd_all[par, ctx] = add_all(gd2[ctx].astype(F32), [gd_r[k] for k in range(C - 1)]).astype(BF)
    cg3 = [
        send(gd_all.at[par, ctx], gd_all.at[par, ctx], "ctx", peer("ctx", k))
        for k in range(1, C)
    ]
    a1 = back_ctx(1, a1)
    wait_all(cg3)
    cg4 = send(gd_all.at[par], gd_all.at[par], "dp", mate)
    a1 = back_dp(1, a1)
    wait_all(a0)
    wait_all(a1)
    cg4.wait_recv()
    for cp in sent:
        cp.wait_send()


def outputs(scale, fin, gd_all, up, qmap_t, kmap_t, o_q, o_k, o_up, o_down, o_loss):
    rank, kw = up.shape
    width = o_q.shape[0]
    body_rows = kw // 128 * width
    r = 2 * body_rows
    low_grad = fin[r : r + rank, :]
    hd_t = jnp.concatenate([qmap_t[...], kmap_t[...]], axis=0)
    o_up[...] = ADAPTER_SCALE * mm(low_grad, hd_t)
    lg_t = low_grad.astype(F32).T.astype(BF)
    upper = ADAPTER_SCALE * mm(lg_t, up[...])
    for h, o in ((0, o_q), (1, o_k)):
        for b in range(kw // 128):
            r0 = h * body_rows + b * width
            c = slice(b * 128, (b + 1) * 128)
            o[:, c] = fin[r0 : r0 + width, :].astype(F32) + upper[h * width : (h + 1) * width, c]
    halves, C, _, pw = gd_all.shape
    for p in range(halves):
        for j in range(C):
            at0 = (p * C + j) * pw
            o_down[:, at0 : at0 + pw] = gd_all[p, j].astype(F32)
    l0 = r + rank
    both = fin[l0 : l0 + 16, :].astype(F32) + fin[l0 + 16 : l0 + 32, :].astype(F32)
    o_loss[...] = both[0:1, 0:1] * scale


def on_device(
    box_hidden_states,
    box_token_positions,
    document_lengths,
    successors,
    fixed_key_matrix,
    adapter_down,
    adapter_up,
    pointer_query_map,
    pointer_key_map,
):
    D, F, C = lax.axis_size("dp"), lax.axis_size("fsdp"), lax.axis_size("ctx")
    h = box_hidden_states[0]
    count, rows_all = h.shape
    RF = fixed_key_matrix.shape[0]
    PC = RF // 2
    kw = fixed_key_matrix.shape[1]
    width = pointer_query_map.shape[1]
    rank = adapter_up.shape[0]
    unit = D * C * 16
    first = kw // 128 * width
    second = -(-(first + rank + 32) // unit) * unit
    total = first + second
    piece = second // D
    part = piece // C
    NS = min(4, PC // 256)
    V = pltpu.VMEM
    n_sent = (
        4 * NS * (F - 1) + 2 * (C - 1) + 2 * (F + F - 1) + (D // 2 - 1) + 2 * (C - 1) + 1
        + 2 * (2 * (D - 1) + 2 * (C - 1) + (F - 1))
    )
    vm = pl.BlockSpec(memory_space=pltpu.VMEM)
    hbm = pl.BlockSpec(memory_space=pl.ANY)
    qmap_t, kmap_t = pointer_query_map.T, pointer_key_map.T
    fin, gd_all = pl.pallas_call(
        functools.partial(kernel, D, F, C, D * F),
        out_shape=(
            jax.ShapeDtypeStruct((total, 128), BF),
            jax.ShapeDtypeStruct((2, C, rank, PC // C), BF),
        ),
        in_specs=[hbm, hbm] + [vm] * 7,
        out_specs=(vm, vm),
        scratch_shapes=[
            V((kw, 2 * width), BF),
            V((count, rows_all), BF),
            V((RF, kw), BF),
            V((rows_all, 2 * width), BF),
            V((count, 2 * width), F32),
            V((count, rank), F32),
            V((count, 2 * width), BF),
            V((2 * width, count), BF),
            V((C, width, count), BF),
            V((count, C * count), BF),
            V((count, 128), F32),
            V((count, 128), F32),
            V((C - 1, width, count), BF),
            V((C - 1, width, count), BF),
            V((2, width, count), BF),
            V((2, F, width, PC), BF),
            V((2, F, width, PC), BF),
            V((2, F, width, PC), F32),
            V((2, F - 1, width, PC), BF),
            V((2, F - 1, width, PC), BF),
            V((2, width, PC), BF),
            V((total, 128), BF),
            V((2, D - 1, piece, 128), BF),
            V((2, piece, 128), BF),
            V((2, C - 1, part, 128), BF),
            V((2, F, part, 128), BF),
            V((C, rank, PC // C), BF),
            V((max(D // 2 - 1, 1), C, rank, PC // C), BF),
            V((C, rank, PC // C), BF),
            V((C - 1, rank, PC // C), BF),
            pltpu.SemaphoreType.DMA((3 + F,)),
            pltpu.SemaphoreType.DMA((n_sent,)),
            pltpu.SemaphoreType.DMA((n_sent,)),
        ],
        compiler_params=pltpu.CompilerParams(
            collective_id=0, has_side_effects=True, vmem_limit_bytes=56 * 1024 * 1024
        ),
    )(
        h, fixed_key_matrix, adapter_down.T, adapter_up, qmap_t, kmap_t,
        box_token_positions, document_lengths, successors,
    )
    grad_q, grad_k, up_grad, down_t, loss = pl.pallas_call(
        functools.partial(outputs, 1.0 / (D * F * count * C)),
        out_shape=(
            jax.ShapeDtypeStruct((width, kw), F32),
            jax.ShapeDtypeStruct((width, kw), F32),
            jax.ShapeDtypeStruct((rank, kw), F32),
            jax.ShapeDtypeStruct((rank, RF), F32),
            jax.ShapeDtypeStruct((1, 1), F32),
        ),
        in_specs=[vm] * 5,
        out_specs=(vm,) * 5,
    )(fin, gd_all, adapter_up, qmap_t, kmap_t)
    return down_t.T, up_grad, grad_q.T, grad_k.T, loss[0, 0]


def solution(mesh):
    in_specs = (
        P(("dp", "fsdp"), "ctx", None),
        P(("dp", "fsdp"), None),
        P(("dp", "fsdp"), None),
        P(("dp", "fsdp"), "ctx"),
        P("fsdp", None),
        P(),
        P(),
        P(),
        P(),
    )
    out_specs = (P("fsdp", None), P(), P(), P(), P())
    return jax.shard_map(
        on_device, mesh=mesh, in_specs=in_specs, out_specs=out_specs, check_vma=False
    )
```
